768 devices in a mesh: vocab: 96 (over z, y), width: 8 (over x, core).
Axes of the slice: x: 4, y: 8, z: 12, core: 2. Of those that a mesh axis runs over, the one named last changes fastest.
Arguments:
- grad_out: bfloat16 [98304, 7168], P(('vocab', 'width')), may hold values from -6 to 6
- token_ids: int32 [98304], P('vocab'), may hold values from 0 to 18431, as said below
- slot_ids: int32 [96, 192], P('vocab'), may hold values from -1 to 18431, as said below
- param: float32 [18432, 7168], P('vocab', 'width'), may hold values from -6 to 6
- moment1: bfloat16 [18432, 7168], P('vocab', 'width'), may hold values from -4 to 4
- moment2: bfloat16 [18432, 7168], P('vocab', 'width'), may hold values from 0.0099487305 to 1
Outputs:
- new_param: float32 [18432, 7168], P('vocab', 'width')
- new_moment1: bfloat16 [18432, 7168], P('vocab', 'width')
- new_moment2: bfloat16 [18432, 7168], P('vocab', 'width')
The draws below stay inside these ranges and needn't reach their ends.
Inputs may be any that keep to these rules, and one draw needn't show every extreme that they name: `token_ids`: every token's id is one of the ids that slot_ids lists in the row of the token's group. `slot_ids`: in row v, entries b * 2 to b * 2 + 1 list distinct ids of block b (ids b * 192 to (b + 1) * 192 - 1), used entries first, -1 for unused ones. In every draw some block has all 2 entries used in every row.
All inputs are finite; a program needn't handle non-finite values.
Results may differ from the reference program's by a relative error of at most 0.024.
Values may be sent and summed in bfloat16 or wider, within the bound.
No kernel may reach another device: no remote copies, remote signals or barrier semaphores. Data moves between devices by JAX's collectives and lax.ppermute only.
A program may use at most 32 MiB of HBM per device.

```python
import math
import jax
import jax.numpy as jnp
from jax import lax

D = 7168
BLOCK_ROWS = 192
GROUP_TOK = 1024
CAP = 2
GROUPS = 96
SLOTS = 192
TOKENS = 98304
VOCAB = 18432


def common_plan(key):
    subkeys = jax.random.split(key, 6)
    ranking = jax.random.permutation(subkeys[0], GROUPS)
    is_hot = (ranking < max(1, GROUPS // 8)).astype(jnp.int32)
    spread = jax.random.randint(subkeys[1], (GROUPS, GROUPS), 0, 3)
    counts = jnp.minimum(CAP, spread + is_hot[None, :])
    counts = jnp.where((ranking == 0)[None, :], CAP, counts)
    group_index = jnp.arange(GROUPS, dtype=jnp.int32)
    coldest = (group_index[:, None] == GROUPS - 1) & (ranking == GROUPS - 1)[None, :]
    counts = jnp.where(coldest, 1, counts)
    counts = counts.at[0, 0].max(1)
    counts = counts.at[0, GROUPS - 1].max(1)
    first_row = jax.random.randint(subkeys[2], (GROUPS, GROUPS), 0, BLOCK_ROWS)
    first_row = first_row.at[0, 0].set(0)
    first_row = first_row.at[0, GROUPS - 1].set(BLOCK_ROWS - 1)
    row_step = jax.random.randint(subkeys[3], (GROUPS, GROUPS), 1, BLOCK_ROWS)
    second_row = (first_row + row_step) % BLOCK_ROWS
    block_base = jnp.arange(GROUPS, dtype=jnp.int32)[None, :] * BLOCK_ROWS
    slot_rows = jnp.stack([first_row, second_row], -1) + block_base[:, :, None]
    is_live = jnp.arange(CAP, dtype=jnp.int32)[None, None, :] < counts[:, :, None]
    slot_list = jnp.where(is_live, slot_rows, -1).reshape(GROUPS, SLOTS)
    block_weight = GROUPS // (ranking + 1) + 1
    weight = (is_live.astype(jnp.int32) * block_weight[None, :, None]).reshape(GROUPS, SLOTS)
    running = jnp.cumsum(weight, axis=1)
    totals = running[:, -1]
    drawn = jax.random.randint(subkeys[4], (GROUPS, GROUP_TOK), 0, totals[:, None])
    chosen = jnp.sum((running[:, None, :] <= drawn[:, :, None]).astype(jnp.int32), axis=2)
    live_flat = is_live.reshape(GROUPS, SLOTS).astype(jnp.int32)
    sort_keys = (1 - live_flat) * SLOTS + jnp.arange(SLOTS, dtype=jnp.int32)[None, :]
    live_order = jnp.argsort(sort_keys, axis=1)
    live_count = jnp.sum(live_flat, axis=1)
    positions = jnp.arange(GROUP_TOK, dtype=jnp.int32)
    ordered = jnp.take_along_axis(live_order, jnp.broadcast_to(jnp.minimum(positions, SLOTS - 1)[None, :], (GROUPS, GROUP_TOK)), axis=1)
    chosen = jnp.where(positions[None, :] < live_count[:, None], ordered, chosen)
    chosen = chosen.at[0, 0].set((GROUPS - 1) * CAP)
    chosen = chosen.at[0, 1].set(0)
    token_ids = jnp.take_along_axis(slot_list, chosen, axis=1)
    token_ids = jax.random.permutation(subkeys[5], token_ids, axis=1, independent=True)
    return (slot_list.astype(jnp.int32), token_ids.reshape(TOKENS).astype(jnp.int32))


def draw_slot_ids(key, part):
    slot_list, token_ids = common_plan(key)
    return slot_list


def draw_token_ids(key, part):
    slot_list, token_ids = common_plan(key)
    return token_ids


def levels(rng, extent, pieces, least, high):
    gain, own = 1.0, jax.random.fold_in(rng, 6)
    for dim, blocks in pieces:
        heights = jnp.exp(jax.random.uniform(jax.random.fold_in(own, dim), (blocks,), jnp.float32, least / len(pieces), high / len(pieces)))
        gain = gain * jnp.repeat(heights, extent[dim] // blocks).reshape([-1 if axis == dim else 1 for axis in range(len(extent))])
    return gain


def normal_values(own_key, dims, deviation, limit, cuts=(), held_as=jnp.bfloat16):
    result = jax.random.normal(own_key, dims, jnp.float32) * deviation
    if len(cuts) > 0:
        result = levels(own_key, dims, cuts, -0.22, 0.18) * result
    return jnp.clip(result, min=-limit, max=limit).astype(held_as)


def setup_inputs(seed: int = 0) -> dict:
    keys = jax.random.split(jax.random.key(seed), 7)
    return {
        "grad_out": normal_values(keys[0], (TOKENS, D), 1.0, 6.0, ((0, 768),)),
        "token_ids": draw_token_ids(jax.random.fold_in(keys[6], 71), 0),
        "slot_ids": draw_slot_ids(jax.random.fold_in(keys[6], 71), 0),
        "param": normal_values(keys[3], (VOCAB, D), 1.0, 6.0, ((0, 96), (1, 8)), jnp.float32),
        "moment1": normal_values(keys[4], (VOCAB, D), 0.3, 4.0, ((0, 96), (1, 8))),
        "moment2": jnp.clip(jnp.exp(math.log(1.0) - 4.61031033 * jax.random.uniform(keys[5], (VOCAB, D), jnp.float32) ** levels(keys[5], (VOCAB, D), ((0, 96), (1, 8)), -0.2, 0.2)), 0.0099487305, 1.0).astype(jnp.bfloat16),
    }


BETA_ONE = 0.9
BETA_TWO = 0.95
LEARN_RATE = 0.01
WEIGHT_DECAY = 0.1
EPSILON = 1e-08
CORRECT_ONE = 1.0 - 0.9 ** 10
CORRECT_TWO = 1.0 - 0.95 ** 10

def adamw_rows(param, moment1, moment2, table_grad):
    first_full = BETA_ONE * moment1.astype(jnp.float32) + (1.0 - BETA_ONE) * table_grad
    second_full = BETA_TWO * moment2.astype(jnp.float32) + (1.0 - BETA_TWO) * table_grad * table_grad
    new_moment1 = lax.optimization_barrier(first_full.astype(jnp.bfloat16))
    new_moment2 = lax.optimization_barrier(second_full.astype(jnp.bfloat16))
    first_round = new_moment1.astype(jnp.float32)
    second_round = new_moment2.astype(jnp.float32)
    update = first_round / CORRECT_ONE / (jnp.sqrt(second_round / CORRECT_TWO) + EPSILON)
    new_param = param - LEARN_RATE * (update + WEIGHT_DECAY * param)
    return (new_param, new_moment1, new_moment2)

def group_sums(packed):
    token_rows, group_ids, slot_list = packed
    onehot = (slot_list[:, None] == group_ids[None, :]).astype(jnp.bfloat16)
    return jnp.dot(onehot, token_rows, preferred_element_type=jnp.float32).astype(jnp.bfloat16)

def owner_update(packed):
    slot_rows, slot_names, owner_index, param_block, first_block, second_block = packed
    local_rows = slot_names - owner_index * BLOCK_ROWS
    onehot = (jnp.arange(BLOCK_ROWS, dtype=jnp.int32)[:, None] == local_rows[None, :]).astype(jnp.bfloat16)
    table_grad = jnp.dot(onehot, slot_rows, preferred_element_type=jnp.float32)
    return adamw_rows(param_block, first_block, second_block, table_grad)

def reference(grad_out, token_ids, slot_ids, param, moment1, moment2):
    grouped = grad_out.reshape(GROUPS, GROUP_TOK, D)
    group_ids = token_ids.reshape(GROUPS, GROUP_TOK)
    slot_sums = lax.map(group_sums, (grouped, group_ids, slot_ids))
    slot_sums = jnp.swapaxes(slot_sums.reshape(GROUPS, GROUPS, CAP, D), 0, 1).reshape(GROUPS, GROUPS * CAP, D)
    targets = jnp.swapaxes(slot_ids.reshape(GROUPS, GROUPS, CAP), 0, 1).reshape(GROUPS, GROUPS * CAP)
    owners = jnp.arange(GROUPS, dtype=jnp.int32)
    block_shape = (GROUPS, BLOCK_ROWS, D)
    new_param, new_moment1, new_moment2 = lax.map(owner_update, (slot_sums, targets, owners, param.reshape(block_shape), moment1.reshape(block_shape), moment2.reshape(block_shape)))
    return (new_param.reshape(VOCAB, D), new_moment1.reshape(VOCAB, D), new_moment2.reshape(VOCAB, D))
```

```python
import functools

import jax
import jax.numpy as jnp
from jax import lax
from jax.experimental import pallas as pl
from jax.experimental.pallas import tpu as pltpu
from jax.sharding import Mesh, PartitionSpec as P

BETA_ONE = 0.9
BETA_TWO = 0.95
LEARN_RATE = 0.01
WEIGHT_DECAY = 0.1
EPSILON = 1e-08
CORRECT_ONE = 1.0 - 0.9**10
CORRECT_TWO = 1.0 - 0.95**10
CAP = 2
LANES = 128


def adamw_rows(param, moment1, moment2, table_grad):
    first_full = BETA_ONE * moment1.astype(jnp.float32) + (1.0 - BETA_ONE) * table_grad
    second_full = (
        BETA_TWO * moment2.astype(jnp.float32) + (1.0 - BETA_TWO) * table_grad * table_grad
    )
    new_moment1 = lax.optimization_barrier(first_full.astype(jnp.bfloat16))
    new_moment2 = lax.optimization_barrier(second_full.astype(jnp.bfloat16))
    first_round = new_moment1.astype(jnp.float32)
    second_round = new_moment2.astype(jnp.float32)
    update = first_round / CORRECT_ONE / (jnp.sqrt(second_round / CORRECT_TWO) + EPSILON)
    new_param = param - LEARN_RATE * (update + WEIGHT_DECAY * param)
    return (new_param, new_moment1, new_moment2)


def chip_sums_kernel(block_rows, tokens_ref, slots_ref, own_ref, other_ref, out_ref, rows_ref, held, sems):
    x, c = lax.axis_index("x"), lax.axis_index("c")
    parts, groups, pair = out_ref.shape
    cols = pair // CAP
    half = own_ref.shape[0]
    copies = []
    for p in range(parts):
        start = pl.multiple_of((2 * p + c) * cols, LANES)
        for h, ref in enumerate((own_ref, other_ref)):
            copy = pltpu.make_async_copy(
                ref.at[:, pl.ds(start, cols)], held.at[p, pl.ds(h * half, half), :], sems.at[p, h]
            )
            copy.start()
            copies.append(copy)
    slots = slots_ref[...]
    wide = jnp.broadcast_to(slots, (groups, slots.shape[1]))
    row = lax.broadcasted_iota(jnp.int32, wide.shape, 0)
    lane = lax.broadcasted_iota(jnp.int32, wide.shape, 1)
    columns = [
        jnp.sum(jnp.where(lane == CAP * row + k, wide, 0), axis=1, keepdims=True) for k in range(CAP)
    ]
    first = 2 * x * half
    own_ids = tokens_ref[:, pl.ds(pl.multiple_of(first + c * half, LANES), half)]
    other_ids = tokens_ref[:, pl.ds(pl.multiple_of(first + (1 - c) * half, LANES), half)]
    ids = jnp.concatenate([own_ids, other_ids], axis=1)
    hots = [(col == ids).astype(jnp.float32).astype(jnp.bfloat16) for col in columns]
    base = lax.broadcasted_iota(jnp.int32, (groups, LANES), 0) * block_rows
    which = lax.broadcasted_iota(jnp.int32, (groups, LANES), 1)
    local = jnp.where(which == 0, columns[0], columns[1])
    local = jnp.where(local < 0, -1, local - base)
    rows_ref[...] = local.astype(jnp.float32).astype(jnp.bfloat16)
    for p in range(parts):
        copies[2 * p].wait()
        copies[2 * p + 1].wait()
        for k in range(CAP):
            out_ref[p, :, k * cols : (k + 1) * cols] = jnp.dot(
                hots[k], held[p], preferred_element_type=jnp.float32
            ).astype(jnp.bfloat16)


def chip_sums(token_ids, slot_ids, own, other, parts, block_rows):
    half, width = own.shape
    cols = width // (2 * parts)
    slots = slot_ids.shape[1]
    groups = slots // CAP
    vmem = pl.BlockSpec(memory_space=pltpu.VMEM)
    hbm = pl.BlockSpec(memory_space=pl.ANY)
    return pl.pallas_call(
        functools.partial(chip_sums_kernel, block_rows),
        out_shape=(
            jax.ShapeDtypeStruct((parts, groups, CAP * cols), jnp.bfloat16),
            jax.ShapeDtypeStruct((groups, LANES), jnp.bfloat16),
        ),
        in_specs=[vmem, vmem, hbm, hbm],
        out_specs=(vmem, vmem),
        scratch_shapes=[
            pltpu.VMEM((parts, 2 * half, cols), jnp.bfloat16),
            pltpu.SemaphoreType.DMA((parts, 2)),
        ],
        compiler_params=pltpu.CompilerParams(vmem_limit_bytes=24 * 1024 * 1024),
    )(token_ids.reshape(1, -1), slot_ids, own, other)


def per_device(grad_out, token_ids, slot_ids, param, moment1, moment2):
    block_rows, cols = param.shape
    parts = grad_out.shape[1] // (2 * cols)
    groups = slot_ids.shape[1] // CAP
    other = lax.ppermute(grad_out, "c", [(0, 1), (1, 0)])
    sums, rows = chip_sums(token_ids, slot_ids, grad_out, other, parts, block_rows)
    arrived = lax.all_to_all(sums, "x", split_axis=0, concat_axis=0, tiled=True)
    total = jnp.sum(arrived.astype(jnp.float32), axis=0).astype(jnp.bfloat16)
    outgoing = jnp.concatenate([total, rows], axis=1)[:, None, :]
    slot_sums = lax.all_to_all(outgoing, "vocab", split_axis=0, concat_axis=0, tiled=True)
    slot_sums = slot_sums.reshape(groups, -1)
    table_grad = jnp.zeros((block_rows, cols), jnp.float32)
    for k in range(CAP):
        named = slot_sums[:, CAP * cols + k].astype(jnp.int32)
        selector = (named[:, None] == lax.iota(jnp.int32, block_rows)[None, :]).astype(jnp.bfloat16)
        table_grad += lax.dot_general(
            selector,
            slot_sums[:, k * cols : (k + 1) * cols],
            (((0,), (0,)), ((), ())),
            preferred_element_type=jnp.float32,
        )
    return adamw_rows(param, moment1, moment2, table_grad)


def solution(mesh):
    vocab, width = mesh.devices.shape
    split = Mesh(mesh.devices.reshape(vocab, width // 2, 2), ("vocab", "x", "c"))
    slab = P("vocab", ("x", "c"))
    return jax.shard_map(
        per_device,
        mesh=split,
        in_specs=(P(("vocab", "x", "c"), None), P("vocab"), P("vocab", None), slab, slab, slab),
        out_specs=(slab, slab, slab),
        check_vma=False,
    )
```

```python
import jax
import jax.numpy as jnp
from jax import lax
from jax.experimental import pallas as pl
from jax.experimental.pallas import tpu as pltpu
from jax.sharding import Mesh, PartitionSpec as P

BETA_ONE = 0.9
BETA_TWO = 0.95
LEARN_RATE = 0.01
WEIGHT_DECAY = 0.1
EPSILON = 1e-08
CORRECT_ONE = 1.0 - 0.9**10
CORRECT_TWO = 1.0 - 0.95**10
CAP = 2
LANES = 128
VMEM = pl.BlockSpec(memory_space=pltpu.VMEM)
HBM = pl.BlockSpec(memory_space=pltpu.HBM)


def one_hot(mask):
    return mask.astype(jnp.float32).astype(jnp.bfloat16)


def setup_kernel(block_rows, tokens_ref, slots_ref, grad_ref, hot_ref, rows_ref, own_ref, tokens, slot_row, sems):
    x, c = lax.axis_index("x"), lax.axis_index("c")
    parts, half, cols = own_ref.shape
    slots = slot_row.shape[1]
    first = pl.multiple_of(2 * x * half, LANES)
    small = [
        pltpu.make_async_copy(tokens_ref.at[:, pl.ds(first, 2 * half)], tokens, sems.at[parts]),
        pltpu.make_async_copy(slots_ref, slot_row, sems.at[parts + 1]),
    ]
    large = []
    for k in range(parts):
        start = pl.multiple_of((2 * lax.rem(x + k, parts) + c) * cols, LANES)
        large.append(pltpu.make_async_copy(grad_ref.at[:, pl.ds(start, cols)], own_ref.at[k], sems.at[k]))
    for copy in small + large:
        copy.start()
    for copy in small:
        copy.wait()
    row = lax.broadcasted_iota(jnp.int32, (slots, slots), 0)
    lane = lax.broadcasted_iota(jnp.int32, (slots, slots), 1)
    wide = jnp.broadcast_to(slot_row[...], (slots, slots))
    column = jnp.sum(jnp.where(lane == row, wide, 0), axis=1, keepdims=True)
    low, high = tokens[:, :half], tokens[:, half:]
    hot_ref[:, :half] = one_hot(column == jnp.where(c == 0, low, high))
    hot_ref[:, half:] = one_hot(column == jnp.where(c == 0, high, low))
    block = lax.broadcasted_iota(jnp.int32, (slots, LANES), 0) // CAP
    local = jnp.where(column < 0, -1, column - block * block_rows)
    rows_ref[...] = local.astype(jnp.float32).astype(jnp.bfloat16)
    for copy in large:
        copy.wait()


def chip_sums_kernel(hot_ref, own_ref, other_ref, *out_refs):
    x, c = lax.axis_index("x"), lax.axis_index("c")
    parts, half, cols = own_ref.shape
    for k in (2, 1, 3, 0) if parts == 4 else range(parts):
        start = pl.multiple_of((2 * lax.rem(x + k, parts) + c) * cols, LANES)
        tokens = jnp.concatenate([own_ref[k], other_ref[:, pl.ds(start, cols)]], axis=0)
        out_refs[k][...] = jnp.dot(hot_ref[...], tokens, preferred_element_type=jnp.float32).astype(jnp.bfloat16)


def group_sums_kernel(rows_ref, *refs):
    parts, out_ref = refs[:-1], refs[-1]
    cols = parts[0].shape[1]
    total = parts[0][...].astype(jnp.float32)
    for ref in parts[1:]:
        total += ref[...].astype(jnp.float32)
    out_ref[:, :cols] = total.astype(jnp.bfloat16)
    out_ref[:, cols:] = rows_ref[...]


def update_kernel(sums_ref, param_ref, first_ref, second_ref, *refs):
    outs, (param_buf, first_buf, second_buf, sems) = refs[:3], refs[3:]
    block_rows, cols = param_ref.shape
    names = sums_ref[:, cols:].astype(jnp.int32)
    row = lax.broadcasted_iota(jnp.int32, names.shape, 1)
    pieces = [one_hot(names == row + start) for start in range(0, block_rows, LANES)]
    selector = jnp.concatenate(pieces, axis=1)
    copies = []
    step = 2 * LANES if cols % (2 * LANES) == 0 else LANES
    step = cols // 7 * 2 if cols % (7 * LANES) == 0 else step
    edges = list(range(0, cols, step)) + [cols]
    for i, (lo, hi) in enumerate(zip(edges[:-1], edges[1:])):
        table_grad = lax.dot_general(
            selector, sums_ref[:, lo:hi], (((0,), (0,)), ((), ())), preferred_element_type=jnp.float32
        )[:block_rows]
        first = BETA_ONE * first_ref[:, lo:hi].astype(jnp.float32) + (1.0 - BETA_ONE) * table_grad
        second = BETA_TWO * second_ref[:, lo:hi].astype(jnp.float32) + (1.0 - BETA_TWO) * table_grad * table_grad
        first, second = first.astype(jnp.bfloat16), second.astype(jnp.bfloat16)
        first_buf[:, lo:hi] = first
        second_buf[:, lo:hi] = second
        scale = jnp.sqrt(second.astype(jnp.float32) * (1.0 / CORRECT_TWO)) + EPSILON
        change = first.astype(jnp.float32) * (1.0 / CORRECT_ONE) / scale
        old = param_ref[:, lo:hi]
        param_buf[:, lo:hi] = old - LEARN_RATE * (change + WEIGHT_DECAY * old)
        for j, (buf, out) in enumerate(zip((param_buf, first_buf, second_buf), outs)):
            copy = pltpu.make_async_copy(buf.at[:, pl.ds(lo, hi - lo)], out.at[:, pl.ds(lo, hi - lo)], sems.at[i, j])
            copy.start()
            copies.append(copy)
    for copy in copies:
        copy.wait()


def per_device(grad_out, token_ids, slot_ids, param, moment1, moment2):
    half = grad_out.shape[0]
    block_rows, cols = param.shape
    parts = grad_out.shape[1] // (2 * cols)
    slots = slot_ids.shape[1]
    bf16, f32 = jnp.bfloat16, jnp.float32
    limit = pltpu.CompilerParams(vmem_limit_bytes=24 * 1024 * 1024)

    other = lax.ppermute(grad_out, "c", [(0, 1), (1, 0)])
    hot, rows, own = pl.pallas_call(
        lambda *refs: setup_kernel(block_rows, *refs),
        out_shape=(
            jax.ShapeDtypeStruct((slots, 2 * half), bf16),
            jax.ShapeDtypeStruct((slots, LANES), bf16),
            jax.ShapeDtypeStruct((parts, half, cols), bf16),
        ),
        in_specs=[HBM] * 3,
        out_specs=(VMEM,) * 3,
        scratch_shapes=[
            pltpu.VMEM((1, 2 * half), jnp.int32),
            pltpu.VMEM((1, slots), jnp.int32),
            pltpu.SemaphoreType.DMA((parts + 2,)),
        ],
        compiler_params=limit,
        cost_estimate=pl.CostEstimate(flops=10**6, bytes_accessed=4 * 10**6, transcendentals=0),
        name="setup",
    )(token_ids.reshape(1, -1), slot_ids, grad_out)
    sums = pl.pallas_call(
        chip_sums_kernel,
        out_shape=(jax.ShapeDtypeStruct((slots, cols), bf16),) * parts,
        in_specs=[VMEM] * 3,
        out_specs=(VMEM,) * parts,
        compiler_params=limit,
        name="chip_sums",
    )(hot, own, other)
    arrived = [sums[0]]
    for k in range(1, parts):
        arrived.append(lax.ppermute(sums[k], "x", [(i, (i + k) % parts) for i in range(parts)]))
    outgoing = pl.pallas_call(
        group_sums_kernel,
        out_shape=jax.ShapeDtypeStruct((slots, cols + LANES), bf16),
        in_specs=[VMEM] * (parts + 1),
        out_specs=VMEM,
        compiler_params=limit,
        name="group_sums",
    )(rows, *arrived)
    outgoing = outgoing.reshape(slots // CAP, CAP, cols + LANES)
    slot_sums = lax.all_to_all(outgoing, "vocab", split_axis=0, concat_axis=0, tiled=True)
    slot_sums = slot_sums.reshape(slots, cols + LANES)
    chunks = 8
    return tuple(
        pl.pallas_call(
            update_kernel,
            out_shape=(
                jax.ShapeDtypeStruct(param.shape, f32),
                jax.ShapeDtypeStruct(param.shape, bf16),
                jax.ShapeDtypeStruct(param.shape, bf16),
            ),
            in_specs=[VMEM] * 4,
            out_specs=(HBM,) * 3,
            scratch_shapes=[
                pltpu.VMEM(param.shape, f32),
                pltpu.VMEM(param.shape, bf16),
                pltpu.VMEM(param.shape, bf16),
                pltpu.SemaphoreType.DMA((chunks, 3)),
            ],
            compiler_params=limit,
            name="update",
        )(slot_sums, param, moment1, moment2)
    )


def solution(mesh):
    vocab, width = mesh.devices.shape
    split = Mesh(mesh.devices.reshape(vocab, width // 2, 2), ("vocab", "x", "c"))
    slab = P("vocab", ("x", "c"))
    return jax.shard_map(
        per_device,
        mesh=split,
        in_specs=(P(("vocab", "x", "c"), None), P("vocab"), P("vocab", None), slab, slab, slab),
        out_specs=(slab, slab, slab),
        check_vma=False,
    )
```

```python
import jax
import jax.numpy as jnp
from jax import lax
from jax.experimental import pallas as pl
from jax.experimental.pallas import tpu as pltpu
from jax.sharding import Mesh, PartitionSpec as P

BETA_ONE = 0.9
BETA_TWO = 0.95
LEARN_RATE = 0.01
WEIGHT_DECAY = 0.1
EPSILON = 1e-08
CORRECT_ONE = 1.0 - 0.9**10
CORRECT_TWO = 1.0 - 0.95**10
CAP = 2
LANES = 128
VMEM = pl.BlockSpec(memory_space=pltpu.VMEM)
HBM = pl.BlockSpec(memory_space=pltpu.HBM)


def one_hot(mask):
    return mask.astype(jnp.float32).astype(jnp.bfloat16)


def chips(parts):
    x, c = lax.axis_index("x"), lax.axis_index("c")
    near, far = x ^ 1, x ^ (parts - 1)
    return c, x, jnp.where(c == 0, near, far), jnp.where(c == 0, far, near), x ^ 2


def block(chip, c, cols):
    return pl.ds(pl.multiple_of((2 * chip + c) * cols, LANES), cols)


def setup_kernel(block_rows, tokens_ref, slots_ref, grad_ref, hot_ref, rows_ref, own_ref, tokens, slot_row, sems):
    parts, half, cols = own_ref.shape
    slots = slot_row.shape[1]
    c, x, partner, later, across = chips(parts)
    first = pl.multiple_of(2 * x * half, LANES)
    small = [
        pltpu.make_async_copy(tokens_ref.at[:, pl.ds(first, 2 * half)], tokens, sems.at[parts]),
        pltpu.make_async_copy(slots_ref, slot_row, sems.at[parts + 1]),
    ]
    large = [
        pltpu.make_async_copy(grad_ref.at[:, block(chip, c, cols)], own_ref.at[k], sems.at[k])
        for k, chip in enumerate((partner, across, x, later))
    ]
    for copy in small + large:
        copy.start()
    for copy in small:
        copy.wait()
    row = lax.broadcasted_iota(jnp.int32, (slots, slots), 0)
    lane = lax.broadcasted_iota(jnp.int32, (slots, slots), 1)
    wide = jnp.broadcast_to(slot_row[...], (slots, slots))
    column = jnp.sum(jnp.where(lane == row, wide, 0), axis=1, keepdims=True)
    low, high = tokens[:, :half], tokens[:, half:]
    hot_ref[:, :half] = one_hot(column == jnp.where(c == 0, low, high))
    hot_ref[:, half:] = one_hot(column == jnp.where(c == 0, high, low))
    owner = lax.broadcasted_iota(jnp.int32, (slots, LANES), 0) // CAP
    local = jnp.where(column < 0, -1, column - owner * block_rows)
    rows_ref[...] = local.astype(jnp.float32).astype(jnp.bfloat16)
    for copy in large:
        copy.wait()


def chip_sums_kernel(keep, hot_ref, own_ref, other_ref, out_ref):
    parts, half, cols = own_ref.shape
    c, x, partner, later, across = chips(parts)
    for k, chip in enumerate((x, later) if keep else (partner, across)):
        tokens = jnp.concatenate([own_ref[2 * keep + k], other_ref[:, block(chip, c, cols)]], axis=0)
        total = jnp.dot(hot_ref[...], tokens, preferred_element_type=jnp.float32)
        out_ref[:, k * cols : (k + 1) * cols] = total.astype(out_ref.dtype)


def pair_sums_kernel(kept_ref, arrived_ref, out_ref):
    cols = out_ref.shape[1]
    out_ref[...] = (kept_ref[:, cols:] + arrived_ref[:, cols:].astype(jnp.float32)).astype(jnp.bfloat16)


def group_sums_kernel(rows_ref, kept_ref, arrived_ref, last_ref, out_ref):
    cols = last_ref.shape[1]
    total = kept_ref[:, :cols] + arrived_ref[:, :cols].astype(jnp.float32) + last_ref[...].astype(jnp.float32)
    out_ref[:, :cols] = total.astype(jnp.bfloat16)
    out_ref[:, cols:] = rows_ref[...]


def update_kernel(sums_ref, param_ref, first_ref, second_ref, *refs):
    outs, (param_buf, first_buf, second_buf, sems) = refs[:3], refs[3:]
    block_rows, cols = param_ref.shape
    names = sums_ref[:, cols:].astype(jnp.int32)
    row = lax.broadcasted_iota(jnp.int32, names.shape, 1)
    pieces = [one_hot(names == row + start) for start in range(0, block_rows, LANES)]
    selector = jnp.concatenate(pieces, axis=1)
    copies = []
    step = 2 * LANES if cols % (2 * LANES) == 0 else LANES
    step = cols // 7 * 2 if cols % (7 * LANES) == 0 else step
    edges = list(range(0, cols, step)) + [cols]
    for i, (lo, hi) in enumerate(zip(edges[:-1], edges[1:])):
        table_grad = lax.dot_general(
            selector, sums_ref[:, lo:hi], (((0,), (0,)), ((), ())), preferred_element_type=jnp.float32
        )[:block_rows]
        first = BETA_ONE * first_ref[:, lo:hi].astype(jnp.float32) + (1.0 - BETA_ONE) * table_grad
        second = BETA_TWO * second_ref[:, lo:hi].astype(jnp.float32) + (1.0 - BETA_TWO) * table_grad * table_grad
        first, second = first.astype(jnp.bfloat16), second.astype(jnp.bfloat16)
        first_buf[:, lo:hi] = first
        second_buf[:, lo:hi] = second
        scale = jnp.sqrt(second.astype(jnp.float32) * (1.0 / CORRECT_TWO)) + EPSILON
        change = first.astype(jnp.float32) * (1.0 / CORRECT_ONE) / scale
        old = param_ref[:, lo:hi]
        param_buf[:, lo:hi] = old - LEARN_RATE * (change + WEIGHT_DECAY * old)
        for j, (buf, out) in enumerate(zip((param_buf, first_buf, second_buf), outs)):
            copy = pltpu.make_async_copy(buf.at[:, pl.ds(lo, hi - lo)], out.at[:, pl.ds(lo, hi - lo)], sems.at[i, j])
            copy.start()
            copies.append(copy)
    for copy in copies:
        copy.wait()


def per_device(grad_out, token_ids, slot_ids, param, moment1, moment2):
    half = grad_out.shape[0]
    block_rows, cols = param.shape
    parts = grad_out.shape[1] // (2 * cols)
    slots = slot_ids.shape[1]
    bf16, f32 = jnp.bfloat16, jnp.float32
    limit = pltpu.CompilerParams(vmem_limit_bytes=24 * 1024 * 1024)

    other = lax.ppermute(grad_out, "c", [(0, 1), (1, 0)])
    hot, rows, own = pl.pallas_call(
        lambda *refs: setup_kernel(block_rows, *refs),
        out_shape=(
            jax.ShapeDtypeStruct((slots, 2 * half), bf16),
            jax.ShapeDtypeStruct((slots, LANES), bf16),
            jax.ShapeDtypeStruct((parts, half, cols), bf16),
        ),
        in_specs=[HBM] * 3,
        out_specs=(VMEM,) * 3,
        scratch_shapes=[
            pltpu.VMEM((1, 2 * half), jnp.int32),
            pltpu.VMEM((1, slots), jnp.int32),
            pltpu.SemaphoreType.DMA((parts + 2,)),
        ],
        compiler_params=limit,
        cost_estimate=pl.CostEstimate(flops=10**6, bytes_accessed=4 * 10**6, transcendentals=0),
        name="setup",
    )(token_ids.reshape(1, -1), slot_ids, grad_out)
    def chip_sums(keep):
        return pl.pallas_call(
            lambda *refs: chip_sums_kernel(keep, *refs),
            out_shape=jax.ShapeDtypeStruct((slots, 2 * cols), f32 if keep else bf16),
            in_specs=[VMEM] * 3,
            out_specs=VMEM,
            compiler_params=limit,
            cost_estimate=pl.CostEstimate(flops=8 * slots * half * cols, bytes_accessed=10**6, transcendentals=0),
            name="chip_sums",
        )(hot, own, other)

    def exchange(values, first):
        places = [(i, c) for i in range(parts) for c in range(2)]
        to = [2 * (i ^ (1 if (c == 0) == first else parts - 1)) + c for i, c in places]
        return lax.ppermute(values, ("x", "c"), list(enumerate(to)))

    arrived = exchange(chip_sums(0), True)
    kept = chip_sums(1)
    outgoing = pl.pallas_call(
        pair_sums_kernel,
        out_shape=jax.ShapeDtypeStruct((slots, cols), bf16),
        in_specs=[VMEM] * 2,
        out_specs=VMEM,
        compiler_params=limit,
        name="pair_sums",
    )(kept, arrived)
    last = exchange(outgoing, False)
    outgoing = pl.pallas_call(
        group_sums_kernel,
        out_shape=jax.ShapeDtypeStruct((slots, cols + LANES), bf16),
        in_specs=[VMEM] * 4,
        out_specs=VMEM,
        compiler_params=limit,
        name="group_sums",
    )(rows, kept, arrived, last)
    outgoing = outgoing.reshape(slots // CAP, CAP, cols + LANES)
    slot_sums = lax.all_to_all(outgoing, "vocab", split_axis=0, concat_axis=0, tiled=True)
    slot_sums = slot_sums.reshape(slots, cols + LANES)
    chunks = 8
    return tuple(
        pl.pallas_call(
            update_kernel,
            out_shape=(
                jax.ShapeDtypeStruct(param.shape, f32),
                jax.ShapeDtypeStruct(param.shape, bf16),
                jax.ShapeDtypeStruct(param.shape, bf16),
            ),
            in_specs=[VMEM] * 4,
            out_specs=(HBM,) * 3,
            scratch_shapes=[
                pltpu.VMEM(param.shape, f32),
                pltpu.VMEM(param.shape, bf16),
                pltpu.VMEM(param.shape, bf16),
                pltpu.SemaphoreType.DMA((chunks, 3)),
            ],
            compiler_params=limit,
            name="update",
        )(slot_sums, param, moment1, moment2)
    )


def solution(mesh):
    vocab, width = mesh.devices.shape
    split = Mesh(mesh.devices.reshape(vocab, width // 2, 2), ("vocab", "x", "c"))
    slab = P("vocab", ("x", "c"))
    return jax.shard_map(
        per_device,
        mesh=split,
        in_specs=(P(("vocab", "x", "c"), None), P("vocab"), P("vocab", None), slab, slab, slab),
        out_specs=(slab, slab, slab),
        check_vma=False,
    )
```

```python
import jax
import jax.numpy as jnp
from jax import lax
from jax.experimental import pallas as pl
from jax.experimental.pallas import tpu as pltpu
from jax.sharding import Mesh, PartitionSpec as P

BETA_ONE = 0.9
BETA_TWO = 0.95
LEARN_RATE = 0.01
WEIGHT_DECAY = 0.1
EPSILON = 1e-08
CORRECT_ONE = 1.0 - 0.9**10
CORRECT_TWO = 1.0 - 0.95**10
CAP = 2
LANES = 128
VMEM = pl.BlockSpec(memory_space=pltpu.VMEM)
HBM = pl.BlockSpec(memory_space=pltpu.HBM)


def one_hot(mask):
    return mask.astype(jnp.float32).astype(jnp.bfloat16)


def chips(parts):
    x, c = lax.axis_index("x"), lax.axis_index("c")
    near, far = x ^ 1, x ^ (parts - 1)
    return c, x, jnp.where(c == 0, near, far), jnp.where(c == 0, far, near), x ^ 2


def block(chip, c, cols):
    return pl.ds(pl.multiple_of((2 * chip + c) * cols, LANES), cols)


def setup_kernel(block_rows, tokens_ref, slots_ref, grad_ref, hot_ref, rows_ref, own_ref, tokens, slot_row, sems):
    parts, half, cols = own_ref.shape
    slots = slot_row.shape[1]
    c, x, partner, later, across = chips(parts)
    first = pl.multiple_of(2 * x * half, LANES)
    small = [
        pltpu.make_async_copy(tokens_ref.at[:, pl.ds(first, 2 * half)], tokens, sems.at[parts]),
        pltpu.make_async_copy(slots_ref, slot_row, sems.at[parts + 1]),
    ]
    large = [
        pltpu.make_async_copy(grad_ref.at[:, block(chip, c, cols)], own_ref.at[k], sems.at[k])
        for k, chip in enumerate((across, partner, x, later))
    ]
    for copy in small + large:
        copy.start()
    for copy in small:
        copy.wait()
    row = lax.broadcasted_iota(jnp.int32, (slots, slots), 0)
    lane = lax.broadcasted_iota(jnp.int32, (slots, slots), 1)
    wide = jnp.broadcast_to(slot_row[...], (slots, slots))
    column = jnp.sum(jnp.where(lane == row, wide, 0), axis=1, keepdims=True)
    low, high = tokens[:, :half], tokens[:, half:]
    hot_ref[:, :half] = one_hot(column == jnp.where(c == 0, low, high))
    hot_ref[:, half:] = one_hot(column == jnp.where(c == 0, high, low))
    owner = lax.broadcasted_iota(jnp.int32, (slots, LANES), 0) // CAP
    local = jnp.where(column < 0, -1, column - owner * block_rows)
    rows_ref[...] = local.astype(jnp.float32).astype(jnp.bfloat16)
    for copy in large:
        copy.wait()


def chip_sums_kernel(which, hot_ref, own_ref, other_ref, *out_refs):
    parts, half, cols = own_ref.shape
    c, x, partner, later, across = chips(parts)
    for k, out_ref in zip(which, out_refs):
        chip = (across, partner, x, later)[k]
        tokens = jnp.concatenate([own_ref[k], other_ref[:, block(chip, c, cols)]], axis=0)
        total = jnp.dot(hot_ref[...], tokens, preferred_element_type=jnp.float32)
        out_ref[...] = total.astype(out_ref.dtype)


def pair_sums_kernel(kept_ref, arrived_ref, out_ref):
    out_ref[...] = (kept_ref[...] + arrived_ref[...].astype(jnp.float32)).astype(jnp.bfloat16)


def group_sums_kernel(rows_ref, kept_ref, arrived_ref, last_ref, out_ref):
    cols = last_ref.shape[1]
    total = kept_ref[...] + arrived_ref[...].astype(jnp.float32) + last_ref[...].astype(jnp.float32)
    out_ref[:, :cols] = total.astype(jnp.bfloat16)
    out_ref[:, cols:] = rows_ref[...]


def update_kernel(sums_ref, param_ref, first_ref, second_ref, *refs):
    outs, (param_buf, first_buf, second_buf, sems) = refs[:3], refs[3:]
    block_rows, cols = param_ref.shape
    names = sums_ref[:, cols:].astype(jnp.int32)
    row = lax.broadcasted_iota(jnp.int32, names.shape, 1)
    pieces = [one_hot(names == row + start) for start in range(0, block_rows, LANES)]
    selector = jnp.concatenate(pieces, axis=1)
    copies = []
    step = 2 * LANES if cols % (2 * LANES) == 0 else LANES
    step = cols // 7 * 2 if cols % (7 * LANES) == 0 else step
    edges = list(range(0, cols, step)) + [cols]
    for i, (lo, hi) in enumerate(zip(edges[:-1], edges[1:])):
        table_grad = lax.dot_general(
            selector, sums_ref[:, lo:hi], (((0,), (0,)), ((), ())), preferred_element_type=jnp.float32
        )[:block_rows]
        first = BETA_ONE * first_ref[:, lo:hi].astype(jnp.float32) + (1.0 - BETA_ONE) * table_grad
        second = BETA_TWO * second_ref[:, lo:hi].astype(jnp.float32) + (1.0 - BETA_TWO) * table_grad * table_grad
        first, second = first.astype(jnp.bfloat16), second.astype(jnp.bfloat16)
        first_buf[:, lo:hi] = first
        second_buf[:, lo:hi] = second
        scale = jnp.sqrt(second.astype(jnp.float32) * (1.0 / CORRECT_TWO)) + EPSILON
        change = first.astype(jnp.float32) * (1.0 / CORRECT_ONE) / scale
        old = param_ref[:, lo:hi]
        param_buf[:, lo:hi] = old - LEARN_RATE * (change + WEIGHT_DECAY * old)
        for j, (buf, out) in enumerate(zip((param_buf, first_buf, second_buf), outs)):
            copy = pltpu.make_async_copy(buf.at[:, pl.ds(lo, hi - lo)], out.at[:, pl.ds(lo, hi - lo)], sems.at[i, j])
            copy.start()
            copies.append(copy)
    for copy in copies:
        copy.wait()


def per_device(grad_out, token_ids, slot_ids, param, moment1, moment2):
    half = grad_out.shape[0]
    block_rows, cols = param.shape
    parts = grad_out.shape[1] // (2 * cols)
    slots = slot_ids.shape[1]
    bf16, f32 = jnp.bfloat16, jnp.float32
    limit = pltpu.CompilerParams(vmem_limit_bytes=24 * 1024 * 1024)

    other = lax.ppermute(grad_out, "c", [(0, 1), (1, 0)])
    hot, rows, own = pl.pallas_call(
        lambda *refs: setup_kernel(block_rows, *refs),
        out_shape=(
            jax.ShapeDtypeStruct((slots, 2 * half), bf16),
            jax.ShapeDtypeStruct((slots, LANES), bf16),
            jax.ShapeDtypeStruct((parts, half, cols), bf16),
        ),
        in_specs=[HBM] * 3,
        out_specs=(VMEM,) * 3,
        scratch_shapes=[
            pltpu.VMEM((1, 2 * half), jnp.int32),
            pltpu.VMEM((1, slots), jnp.int32),
            pltpu.SemaphoreType.DMA((parts + 2,)),
        ],
        compiler_params=limit,
        cost_estimate=pl.CostEstimate(flops=10**6, bytes_accessed=4 * 10**6, transcendentals=0),
        name="setup",
    )(token_ids.reshape(1, -1), slot_ids, grad_out)
    def chip_sums(which, dtype):
        outs = tuple(jax.ShapeDtypeStruct((slots, cols), dtype) for k in which)
        return pl.pallas_call(
            lambda *refs: chip_sums_kernel(which, *refs),
            out_shape=outs,
            in_specs=[VMEM] * 3,
            out_specs=(VMEM,) * len(which),
            compiler_params=limit,
            cost_estimate=pl.CostEstimate(flops=8 * slots * half * cols, bytes_accessed=10**6, transcendentals=0),
            name="chip_sums",
        )(hot, own, other)

    def exchange(values, first):
        places = [(i, c) for i in range(parts) for c in range(2)]
        to = [2 * (i ^ (1 if (c == 0) == first else parts - 1)) + c for i, c in places]
        return lax.ppermute(values, ("x", "c"), list(enumerate(to)))

    first = exchange(*chip_sums((0,), bf16), True)
    second = exchange(*chip_sums((1,), bf16), True)
    kept, passing = chip_sums((2, 3), f32)
    outgoing = pl.pallas_call(
        pair_sums_kernel,
        out_shape=jax.ShapeDtypeStruct((slots, cols), bf16),
        in_specs=[VMEM] * 2,
        out_specs=VMEM,
        compiler_params=limit,
        name="pair_sums",
    )(passing, first)
    last = exchange(outgoing, False)
    outgoing = pl.pallas_call(
        group_sums_kernel,
        out_shape=jax.ShapeDtypeStruct((slots, cols + LANES), bf16),
        in_specs=[VMEM] * 4,
        out_specs=VMEM,
        compiler_params=limit,
        name="group_sums",
    )(rows, kept, second, last)
    outgoing = outgoing.reshape(slots // CAP, CAP, cols + LANES)
    slot_sums = lax.all_to_all(outgoing, "vocab", split_axis=0, concat_axis=0, tiled=True)
    slot_sums = slot_sums.reshape(slots, cols + LANES)
    chunks = 8
    return tuple(
        pl.pallas_call(
            update_kernel,
            out_shape=(
                jax.ShapeDtypeStruct(param.shape, f32),
                jax.ShapeDtypeStruct(param.shape, bf16),
                jax.ShapeDtypeStruct(param.shape, bf16),
            ),
            in_specs=[VMEM] * 4,
            out_specs=(HBM,) * 3,
            scratch_shapes=[
                pltpu.VMEM(param.shape, f32),
                pltpu.VMEM(param.shape, bf16),
                pltpu.VMEM(param.shape, bf16),
                pltpu.SemaphoreType.DMA((chunks, 3)),
            ],
            compiler_params=limit,
            name="update",
        )(slot_sums, param, moment1, moment2)
    )


def solution(mesh):
    vocab, width = mesh.devices.shape
    split = Mesh(mesh.devices.reshape(vocab, width // 2, 2), ("vocab", "x", "c"))
    slab = P("vocab", ("x", "c"))
    return jax.shard_map(
        per_device,
        mesh=split,
        in_specs=(P(("vocab", "x", "c"), None), P("vocab"), P("vocab", None), slab, slab, slab),
        out_specs=(slab, slab, slab),
        check_vma=False,
    )
```

```python
import jax
import jax.numpy as jnp
from jax import lax
from jax.experimental import pallas as pl
from jax.experimental.pallas import tpu as pltpu
from jax.sharding import Mesh, PartitionSpec as P

BETA_ONE = 0.9
BETA_TWO = 0.95
LEARN_RATE = 0.01
WEIGHT_DECAY = 0.1
EPSILON = 1e-08
CORRECT_ONE = 1.0 - 0.9**10
CORRECT_TWO = 1.0 - 0.95**10
CAP = 2
SPREAD = (35, 30)
LANES = 128
VMEM = pl.BlockSpec(memory_space=pltpu.VMEM)
HBM = pl.BlockSpec(memory_space=pltpu.HBM)


def member(place, groups):
    return place * (SPREAD[0] + SPREAD[1] * place) % groups


def one_hot(mask):
    return mask.astype(jnp.float32).astype(jnp.bfloat16)


def chips(parts):
    x, c = lax.axis_index("x"), lax.axis_index("c")
    near, far = x ^ 1, x ^ (parts - 1)
    return c, x, jnp.where(c == 0, near, far), jnp.where(c == 0, far, near), x ^ 2


def block(chip, c, cols):
    return pl.ds(pl.multiple_of((2 * chip + c) * cols, LANES), cols)


def setup_kernel(block_rows, tokens_ref, slots_ref, grad_ref, hot_ref, rows_ref, own_ref, tokens, slot_row, sems):
    parts, half, cols = own_ref.shape
    slots = slot_row.shape[1]
    c, x, partner, later, across = chips(parts)
    first = pl.multiple_of(2 * x * half, LANES)
    small = [
        pltpu.make_async_copy(tokens_ref.at[:, pl.ds(first, 2 * half)], tokens, sems.at[parts]),
        pltpu.make_async_copy(slots_ref, slot_row, sems.at[parts + 1]),
    ]
    large = [
        pltpu.make_async_copy(grad_ref.at[:, block(chip, c, cols)], own_ref.at[k], sems.at[k])
        for k, chip in enumerate((across, partner, x, later))
    ]
    for copy in small + large:
        copy.start()
    for copy in small:
        copy.wait()
    row = lax.broadcasted_iota(jnp.int32, (slots, LANES), 0)
    owner = member(row // CAP, slots // CAP)
    source = jnp.broadcast_to((CAP * owner + row % CAP)[:, :1], (slots, slots))
    lane = lax.broadcasted_iota(jnp.int32, (slots, slots), 1)
    wide = jnp.broadcast_to(slot_row[...], (slots, slots))
    column = jnp.sum(jnp.where(lane == source, wide, 0), axis=1, keepdims=True)
    low, high = tokens[:, :half], tokens[:, half:]
    hot_ref[:, :half] = one_hot(column == jnp.where(c == 0, low, high))
    hot_ref[:, half:] = one_hot(column == jnp.where(c == 0, high, low))
    local = jnp.where(column < 0, -1, column - owner * block_rows)
    rows_ref[...] = local.astype(jnp.float32).astype(jnp.bfloat16)
    for copy in large:
        copy.wait()


def chip_sums_kernel(which, hot_ref, own_ref, other_ref, *out_refs):
    parts, half, cols = own_ref.shape
    c, x, partner, later, across = chips(parts)
    for k, out_ref in zip(which, out_refs):
        chip = (across, partner, x, later)[k]
        tokens = jnp.concatenate([own_ref[k], other_ref[:, block(chip, c, cols)]], axis=0)
        total = jnp.dot(hot_ref[...], tokens, preferred_element_type=jnp.float32)
        out_ref[...] = total.astype(out_ref.dtype)


def pair_sums_kernel(kept_ref, arrived_ref, out_ref):
    out_ref[...] = (kept_ref[...] + arrived_ref[...].astype(jnp.float32)).astype(jnp.bfloat16)


def group_sums_kernel(rows_ref, kept_ref, arrived_ref, last_ref, out_ref):
    cols = last_ref.shape[1]
    total = kept_ref[...] + arrived_ref[...].astype(jnp.float32) + last_ref[...].astype(jnp.float32)
    out_ref[:, :cols] = total.astype(jnp.bfloat16)
    out_ref[:, cols:] = rows_ref[...]


def update_kernel(sums_ref, param_ref, first_ref, second_ref, *refs):
    outs, (param_buf, first_buf, second_buf, sems) = refs[:3], refs[3:]
    block_rows, cols = param_ref.shape
    names = sums_ref[:, cols:].astype(jnp.float32).T
    row = lax.broadcasted_iota(jnp.int32, names.shape, 0).astype(jnp.float32)
    pieces = [one_hot(names == row + start) for start in range(0, block_rows, LANES)]
    selector = jnp.concatenate(pieces, axis=0)[:block_rows]
    copies = []
    step = 2 * LANES if cols % (2 * LANES) == 0 else LANES
    step = cols // 7 * 2 if cols % (7 * LANES) == 0 else step
    edges = list(range(0, cols, step)) + [cols]
    for i, (lo, hi) in enumerate(zip(edges[:-1], edges[1:])):
        table_grad = jnp.dot(selector, sums_ref[:, lo:hi], preferred_element_type=jnp.float32)
        first = BETA_ONE * first_ref[:, lo:hi].astype(jnp.float32) + (1.0 - BETA_ONE) * table_grad
        second = BETA_TWO * second_ref[:, lo:hi].astype(jnp.float32) + (1.0 - BETA_TWO) * table_grad * table_grad
        first, second = first.astype(jnp.bfloat16), second.astype(jnp.bfloat16)
        first_buf[:, lo:hi] = first
        second_buf[:, lo:hi] = second
        square = second.astype(jnp.float32) * (1.0 / CORRECT_TWO)
        scale = pl.reciprocal(square * lax.rsqrt(square) + EPSILON)
        change = first.astype(jnp.float32) * (LEARN_RATE / CORRECT_ONE) * scale
        param_buf[:, lo:hi] = param_ref[:, lo:hi] * (1.0 - LEARN_RATE * WEIGHT_DECAY) - change
        for j, (buf, out) in enumerate(zip((param_buf, first_buf, second_buf), outs)):
            copy = pltpu.make_async_copy(buf.at[:, pl.ds(lo, hi - lo)], out.at[:, pl.ds(lo, hi - lo)], sems.at[i, j])
            copy.start()
            copies.append(copy)
    for copy in copies:
        copy.wait()


def per_device(grad_out, token_ids, slot_ids, param, moment1, moment2):
    half = grad_out.shape[0]
    block_rows, cols = param.shape
    parts = grad_out.shape[1] // (2 * cols)
    slots = slot_ids.shape[1]
    bf16, f32 = jnp.bfloat16, jnp.float32
    limit = pltpu.CompilerParams(vmem_limit_bytes=24 * 1024 * 1024)

    other = lax.ppermute(grad_out, "c", [(0, 1), (1, 0)])
    hot, rows, own = pl.pallas_call(
        lambda *refs: setup_kernel(block_rows, *refs),
        out_shape=(
            jax.ShapeDtypeStruct((slots, 2 * half), bf16),
            jax.ShapeDtypeStruct((slots, LANES), bf16),
            jax.ShapeDtypeStruct((parts, half, cols), bf16),
        ),
        in_specs=[HBM] * 3,
        out_specs=(VMEM,) * 3,
        scratch_shapes=[
            pltpu.VMEM((1, 2 * half), jnp.int32),
            pltpu.VMEM((1, slots), jnp.int32),
            pltpu.SemaphoreType.DMA((parts + 2,)),
        ],
        compiler_params=limit,
        cost_estimate=pl.CostEstimate(flops=10**6, bytes_accessed=4 * 10**6, transcendentals=0),
        name="setup",
    )(token_ids.reshape(1, -1), slot_ids, grad_out)
    def chip_sums(which, dtype):
        outs = tuple(jax.ShapeDtypeStruct((slots, cols), dtype) for k in which)
        return pl.pallas_call(
            lambda *refs: chip_sums_kernel(which, *refs),
            out_shape=outs,
            in_specs=[VMEM] * 3,
            out_specs=(VMEM,) * len(which),
            compiler_params=limit,
            cost_estimate=pl.CostEstimate(flops=8 * slots * half * cols, bytes_accessed=10**6, transcendentals=0),
            name="chip_sums",
        )(hot, own, other)

    def exchange(values, first):
        places = [(i, c) for i in range(parts) for c in range(2)]
        to = [2 * (i ^ (1 if (c == 0) == first else parts - 1)) + c for i, c in places]
        return lax.ppermute(values, ("x", "c"), list(enumerate(to)))

    first = exchange(*chip_sums((0,), bf16), True)
    second = exchange(*chip_sums((1,), bf16), True)
    kept, passing = chip_sums((2, 3), f32)
    outgoing = pl.pallas_call(
        pair_sums_kernel,
        out_shape=jax.ShapeDtypeStruct((slots, cols), bf16),
        in_specs=[VMEM] * 2,
        out_specs=VMEM,
        compiler_params=limit,
        name="pair_sums",
    )(passing, first)
    last = exchange(outgoing, False)
    outgoing = pl.pallas_call(
        group_sums_kernel,
        out_shape=jax.ShapeDtypeStruct((slots, cols + LANES), bf16),
        in_specs=[VMEM] * 4,
        out_specs=VMEM,
        compiler_params=limit,
        name="group_sums",
    )(rows, kept, second, last)
    outgoing = outgoing.reshape(slots // CAP, CAP, cols + LANES)
    groups = slots // CAP
    order = [member(place, groups) for place in range(groups)]
    slot_sums = lax.all_to_all(
        outgoing, "vocab", split_axis=0, concat_axis=0, axis_index_groups=[order], tiled=True
    )
    slot_sums = slot_sums.reshape(slots, cols + LANES)
    chunks = 8
    return tuple(
        pl.pallas_call(
            update_kernel,
            out_shape=(
                jax.ShapeDtypeStruct(param.shape, f32),
                jax.ShapeDtypeStruct(param.shape, bf16),
                jax.ShapeDtypeStruct(param.shape, bf16),
            ),
            in_specs=[VMEM] * 4,
            out_specs=(HBM,) * 3,
            scratch_shapes=[
                pltpu.VMEM(param.shape, f32),
                pltpu.VMEM(param.shape, bf16),
                pltpu.VMEM(param.shape, bf16),
                pltpu.SemaphoreType.DMA((chunks, 3)),
            ],
            compiler_params=limit,
            name="update",
        )(slot_sums, param, moment1, moment2)
    )


def solution(mesh):
    vocab, width = mesh.devices.shape
    split = Mesh(mesh.devices.reshape(vocab, width // 2, 2), ("vocab", "x", "c"))
    slab = P("vocab", ("x", "c"))
    return jax.shard_map(
        per_device,
        mesh=split,
        in_specs=(P(("vocab", "x", "c"), None), P("vocab"), P("vocab", None), slab, slab, slab),
        out_specs=(slab, slab, slab),
        check_vma=False,
    )
```

```python
import jax
import jax.numpy as jnp
from jax import lax
from jax.experimental import pallas as pl
from jax.experimental.pallas import tpu as pltpu
from jax.sharding import Mesh, PartitionSpec as P
import numpy as np

BETA_ONE = 0.9
BETA_TWO = 0.95
LEARN_RATE = 0.01
WEIGHT_DECAY = 0.1
EPSILON = 1e-08
CORRECT_ONE = 1.0 - 0.9**10
CORRECT_TWO = 1.0 - 0.95**10
CAP = 2
LANES = 128
VMEM = pl.BlockSpec(memory_space=pltpu.VMEM)
HBM = pl.BlockSpec(memory_space=pltpu.HBM)


def member_order(groups):
    return np.random.RandomState(3).permutation(groups).tolist()


def one_hot(mask):
    return mask.astype(jnp.float32).astype(jnp.bfloat16)


def chips(parts):
    x, c = lax.axis_index("x"), lax.axis_index("c")
    near, far = x ^ 1, x ^ (parts - 1)
    return c, x, jnp.where(c == 0, near, far), jnp.where(c == 0, far, near), x ^ 2


def block(chip, c, cols):
    return pl.ds(pl.multiple_of((2 * chip + c) * cols, LANES), cols)


def setup_kernel(block_rows, tokens_ref, slots_ref, grad_ref, hot_ref, rows_ref, own_ref, tokens, slot_row, sems):
    parts, half, cols = own_ref.shape
    slots = slot_row.shape[1]
    c, x, partner, later, across = chips(parts)
    first = pl.multiple_of(2 * x * half, LANES)
    small = [
        pltpu.make_async_copy(tokens_ref.at[:, pl.ds(first, 2 * half)], tokens, sems.at[parts]),
        pltpu.make_async_copy(slots_ref, slot_row, sems.at[parts + 1]),
    ]
    large = [
        pltpu.make_async_copy(grad_ref.at[:, block(chip, c, cols)], own_ref.at[k], sems.at[k])
        for k, chip in enumerate((across, partner, x, later))
    ]
    for copy in small + large:
        copy.start()
    for copy in small:
        copy.wait()
    place = lax.broadcasted_iota(jnp.int32, (1, slots), 1) // CAP
    owner_row = jnp.zeros((1, slots), jnp.int32)
    for i, member in enumerate(member_order(slots // CAP)):
        owner_row = jnp.where(place == i, member, owner_row)
    row = lax.broadcasted_iota(jnp.int32, (slots, slots), 0)
    lane = lax.broadcasted_iota(jnp.int32, (slots, slots), 1)
    wide = jnp.broadcast_to(owner_row, (slots, slots))
    owner = jnp.sum(jnp.where(lane == row, wide, 0), axis=1, keepdims=True)
    wide = jnp.broadcast_to(slot_row[...], (slots, slots))
    column = jnp.sum(jnp.where(lane == CAP * owner + row % CAP, wide, 0), axis=1, keepdims=True)
    low, high = tokens[:, :half], tokens[:, half:]
    hot_ref[:, :half] = one_hot(column == jnp.where(c == 0, low, high))
    hot_ref[:, half:] = one_hot(column == jnp.where(c == 0, high, low))
    local = jnp.where(column < 0, -1, column - owner * block_rows)
    local = jnp.broadcast_to(local, (slots, LANES))
    rows_ref[...] = local.astype(jnp.float32).astype(jnp.bfloat16)
    for copy in large:
        copy.wait()


def chip_sums_kernel(which, hot_ref, own_ref, other_ref, *out_refs):
    parts, half, cols = own_ref.shape
    c, x, partner, later, across = chips(parts)
    for k, out_ref in zip(which, out_refs):
        chip = (across, partner, x, later)[k]
        tokens = jnp.concatenate([own_ref[k], other_ref[:, block(chip, c, cols)]], axis=0)
        total = jnp.dot(hot_ref[...], tokens, preferred_element_type=jnp.float32)
        out_ref[...] = total.astype(out_ref.dtype)


def pair_sums_kernel(kept_ref, arrived_ref, out_ref):
    out_ref[...] = (kept_ref[...] + arrived_ref[...].astype(jnp.float32)).astype(jnp.bfloat16)


def group_sums_kernel(rows_ref, kept_ref, arrived_ref, last_ref, out_ref):
    cols = last_ref.shape[1]
    total = kept_ref[...] + arrived_ref[...].astype(jnp.float32) + last_ref[...].astype(jnp.float32)
    out_ref[:, :cols] = total.astype(jnp.bfloat16)
    out_ref[:, cols:] = rows_ref[...]


def update_kernel(sums_ref, param_ref, first_ref, second_ref, *refs):
    outs, (param_buf, first_buf, second_buf, sems) = refs[:3], refs[3:]
    block_rows, cols = param_ref.shape
    names = sums_ref[:, cols:].astype(jnp.float32).T
    row = lax.broadcasted_iota(jnp.int32, names.shape, 0).astype(jnp.float32)
    pieces = [one_hot(names == row + start) for start in range(0, block_rows, LANES)]
    selector = jnp.concatenate(pieces, axis=0)[:block_rows]
    copies = []
    step = 2 * LANES if cols % (2 * LANES) == 0 else LANES
    step = cols // 7 * 2 if cols % (7 * LANES) == 0 else step
    edges = list(range(0, cols, step)) + [cols]
    for i, (lo, hi) in enumerate(zip(edges[:-1], edges[1:])):
        table_grad = jnp.dot(selector, sums_ref[:, lo:hi], preferred_element_type=jnp.float32)
        first = BETA_ONE * first_ref[:, lo:hi].astype(jnp.float32) + (1.0 - BETA_ONE) * table_grad
        second = BETA_TWO * second_ref[:, lo:hi].astype(jnp.float32) + (1.0 - BETA_TWO) * table_grad * table_grad
        first, second = first.astype(jnp.bfloat16), second.astype(jnp.bfloat16)
        first_buf[:, lo:hi] = first
        second_buf[:, lo:hi] = second
        square = second.astype(jnp.float32) * (1.0 / CORRECT_TWO)
        scale = pl.reciprocal(square * lax.rsqrt(square) + EPSILON)
        change = first.astype(jnp.float32) * (LEARN_RATE / CORRECT_ONE) * scale
        param_buf[:, lo:hi] = param_ref[:, lo:hi] * (1.0 - LEARN_RATE * WEIGHT_DECAY) - change
        for j, (buf, out) in enumerate(zip((param_buf, first_buf, second_buf), outs)):
            copy = pltpu.make_async_copy(buf.at[:, pl.ds(lo, hi - lo)], out.at[:, pl.ds(lo, hi - lo)], sems.at[i, j])
            copy.start()
            copies.append(copy)
    for copy in copies:
        copy.wait()


def per_device(grad_out, token_ids, slot_ids, param, moment1, moment2):
    half = grad_out.shape[0]
    block_rows, cols = param.shape
    parts = grad_out.shape[1] // (2 * cols)
    slots = slot_ids.shape[1]
    bf16, f32 = jnp.bfloat16, jnp.float32
    limit = pltpu.CompilerParams(vmem_limit_bytes=24 * 1024 * 1024)

    other = lax.ppermute(grad_out, "c", [(0, 1), (1, 0)])
    hot, rows, own = pl.pallas_call(
        lambda *refs: setup_kernel(block_rows, *refs),
        out_shape=(
            jax.ShapeDtypeStruct((slots, 2 * half), bf16),
            jax.ShapeDtypeStruct((slots, LANES), bf16),
            jax.ShapeDtypeStruct((parts, half, cols), bf16),
        ),
        in_specs=[HBM] * 3,
        out_specs=(VMEM,) * 3,
        scratch_shapes=[
            pltpu.VMEM((1, 2 * half), jnp.int32),
            pltpu.VMEM((1, slots), jnp.int32),
            pltpu.SemaphoreType.DMA((parts + 2,)),
        ],
        compiler_params=limit,
        cost_estimate=pl.CostEstimate(flops=10**6, bytes_accessed=4 * 10**6, transcendentals=0),
        name="setup",
    )(token_ids.reshape(1, -1), slot_ids, grad_out)
    def chip_sums(which, dtype):
        outs = tuple(jax.ShapeDtypeStruct((slots, cols), dtype) for k in which)
        return pl.pallas_call(
            lambda *refs: chip_sums_kernel(which, *refs),
            out_shape=outs,
            in_specs=[VMEM] * 3,
            out_specs=(VMEM,) * len(which),
            compiler_params=limit,
            cost_estimate=pl.CostEstimate(flops=8 * slots * half * cols, bytes_accessed=10**6, transcendentals=0),
            name="chip_sums",
        )(hot, own, other)

    def exchange(values, first):
        places = [(i, c) for i in range(parts) for c in range(2)]
        to = [2 * (i ^ (1 if (c == 0) == first else parts - 1)) + c for i, c in places]
        return lax.ppermute(values, ("x", "c"), list(enumerate(to)))

    first = exchange(*chip_sums((0,), bf16), True)
    second = exchange(*chip_sums((1,), bf16), True)
    kept, passing = chip_sums((2, 3), f32)
    outgoing = pl.pallas_call(
        pair_sums_kernel,
        out_shape=jax.ShapeDtypeStruct((slots, cols), bf16),
        in_specs=[VMEM] * 2,
        out_specs=VMEM,
        compiler_params=limit,
        name="pair_sums",
    )(passing, first)
    last = exchange(outgoing, False)
    outgoing = pl.pallas_call(
        group_sums_kernel,
        out_shape=jax.ShapeDtypeStruct((slots, cols + LANES), bf16),
        in_specs=[VMEM] * 4,
        out_specs=VMEM,
        compiler_params=limit,
        name="group_sums",
    )(rows, kept, second, last)
    outgoing = outgoing.reshape(slots // CAP, CAP, cols + LANES)
    groups = slots // CAP
    order = member_order(groups)
    slot_sums = lax.all_to_all(
        outgoing, "vocab", split_axis=0, concat_axis=0, axis_index_groups=[order], tiled=True
    )
    slot_sums = slot_sums.reshape(slots, cols + LANES)
    chunks = 8
    return tuple(
        pl.pallas_call(
            update_kernel,
            out_shape=(
                jax.ShapeDtypeStruct(param.shape, f32),
                jax.ShapeDtypeStruct(param.shape, bf16),
                jax.ShapeDtypeStruct(param.shape, bf16),
            ),
            in_specs=[VMEM] * 4,
            out_specs=(HBM,) * 3,
            scratch_shapes=[
                pltpu.VMEM(param.shape, f32),
                pltpu.VMEM(param.shape, bf16),
                pltpu.VMEM(param.shape, bf16),
                pltpu.SemaphoreType.DMA((chunks, 3)),
            ],
            compiler_params=limit,
            name="update",
        )(slot_sums, param, moment1, moment2)
    )


def solution(mesh):
    vocab, width = mesh.devices.shape
    split = Mesh(mesh.devices.reshape(vocab, width // 2, 2), ("vocab", "x", "c"))
    slab = P("vocab", ("x", "c"))
    return jax.shard_map(
        per_device,
        mesh=split,
        in_specs=(P(("vocab", "x", "c"), None), P("vocab"), P("vocab", None), slab, slab, slab),
        out_specs=(slab, slab, slab),
        check_vma=False,
    )
```
